256 devices in a mesh: ctx: 64 (over z, x, core), kv: 4 (over y).
Axes of the slice: x: 4, y: 4, z: 8, core: 2. Of those that a mesh axis runs over, the one named last changes fastest.
Arguments:
- queries: bfloat16 [32768, 4096], P(('ctx', 'kv')), may hold values from -162 to 162
- keys: bfloat16 [32768, 512], P(('ctx', 'kv')), may hold values from -6 to 6
- values: bfloat16 [32768, 512], P(('ctx', 'kv')), may hold values from -6 to 6
- grad_out: bfloat16 [32768, 4096], P(('ctx', 'kv')), may hold values from -6 to 6
- doc_lengths: int32 [64], replicated, may hold values from 1 to 1024, 32768 in all
Outputs:
- query_grad: bfloat16 [32768, 4096], P(('ctx', 'kv'))
- key_grad: bfloat16 [32768, 512], P(('ctx', 'kv'))
- value_grad: bfloat16 [32768, 512], P(('ctx', 'kv'))
The draws below stay inside these ranges and needn't reach their ends.
Inputs may be any that keep to these rules, and one draw needn't show every extreme that they name: `doc_lengths`: 64 document lengths in sequence order; they sum to 32768 and the longest is exactly 1024.
All inputs are finite; a program needn't handle non-finite values.
Results may differ from the reference program's by a relative error of at most 0.0055.
Values may be sent and summed in bfloat16 or wider, within the bound.
No kernel may reach another device: no remote copies, remote signals or barrier semaphores. Data moves between devices by JAX's collectives and lax.ppermute only.
A program may use at most 128 MiB of HBM per device.

```python
import math
import jax
import jax.numpy as jnp
import numpy as np
from jax import lax

HD = 128
QG = 8
CH = 256
KH = 4
QH = 32
TOKENS = 32768
SPAN = 4
DOC_MAX = 1024
NDOCS = 64
N_CTX = 64


def shared_rows(key):
    base_keys = jnp.clip(jax.random.normal(jax.random.fold_in(key, 11), (TOKENS, KH * HD), jnp.float32), -6.0, 6.0)
    return base_keys


def draw_keys(key, part):
    base_keys = shared_rows(key)
    return base_keys.astype(jnp.bfloat16)


def draw_queries(key, part):
    key = jax.random.fold_in(key, 5)
    drawn_draw = jax.random.normal(jax.random.fold_in(key, 1), (TOKENS, QH * HD), jnp.float32)
    return jnp.clip(drawn_draw, -6.0, 6.0).astype(jnp.bfloat16)


def steps_of(rng, extent, shards, least, high):
    def one(position, parts):
        steps = jax.random.uniform(jax.random.fold_in(jax.random.fold_in(rng, 6), position), (parts,), jnp.float32, least / len(shards), high / len(shards))
        return jnp.repeat(jnp.exp(steps), extent[position] // parts).reshape((-1,) + (1,) * (len(extent) - position - 1))

    gain = one(*shards[0])
    for cut in shards[1:]:
        gain = gain * one(*cut)
    return gain


def split_up(number_of, total, limit, slope):
    portions = [(1 << 20) // math.isqrt(standing ** slope) + 1 for standing in range(2, number_of + 1)]
    surplus, counts = total - limit - (number_of - 1), [1] * (number_of - 1)
    while surplus > 0:
        movable = [i for i in range(number_of - 1) if counts[i] < limit]
        pool, remaining = sum([portions[i] for i in movable]), surplus
        for i in movable:
            addition = min(limit - counts[i], max(1, remaining * portions[i] // pool), surplus)
            counts[i] = counts[i] + addition
            surplus = surplus - addition
    return np.array([limit] + counts)


def uneven_parts(rng, count, total, limit, slope):
    if count == 2:
        one = jax.random.randint(rng, (), max(1, total - limit), min(limit, total - 1) + 1)
        return jnp.stack([one, total - one])
    tallies = jnp.asarray(split_up(count, total, limit, slope), jnp.int32)
    pairs = (count - 1) // 2
    giver, taker = tallies[1:1 + 2 * pairs:2], tallies[2:2 + 2 * pairs:2]
    room = jnp.minimum(giver - 1, limit - taker)
    shifted = jax.random.randint(jax.random.fold_in(rng, 1), (pairs,), 0, 1 << 20) % (room + 1)
    tallies = tallies.at[1:1 + 2 * pairs:2].set(giver - shifted).at[2:2 + 2 * pairs:2].set(taker + shifted)
    return tallies[jax.random.permutation(jax.random.fold_in(rng, 2), count)]


def bell_draw(own_key, shape, scale, bound, pieces=(), kind=jnp.bfloat16):
    array = scale * jax.random.normal(own_key, shape, jnp.float32)
    if pieces:
        array = array * steps_of(own_key, shape, pieces, -0.22, 0.18)
    return jnp.clip(array, -bound, bound).astype(kind)


def setup_inputs(seed: int = 0) -> dict:
    key_of = jax.random.split(jax.random.key(seed), 6)
    queries = draw_queries(jax.random.fold_in(key_of[5], 71), 0)
    keys = draw_keys(jax.random.fold_in(key_of[5], 71), 0)
    values = bell_draw(key_of[2], (TOKENS, KH * HD), 1.0, 6.0, ((0, 256),))
    grad_out = bell_draw(key_of[3], (TOKENS, QH * HD), 1.0, 6.0, ((0, 256),))
    doc_lengths = uneven_parts(key_of[4], NDOCS, TOKENS, DOC_MAX, 2).astype(jnp.int32)
    return dict(queries=queries, keys=keys, values=values, grad_out=grad_out, doc_lengths=doc_lengths)


MASKED_SCORE = -1e+30

def reference(queries, keys, values, grad_out, doc_lengths):
    row_count = queries.shape[0]
    block_count = row_count // CH
    pad_rows = SPAN * CH
    window_rows = (SPAN + 1) * CH
    score_scale = 1.0 / math.sqrt(HD)
    seq_pos = jnp.arange(row_count, dtype=jnp.int32)
    seq_block = seq_pos // CH
    owner_dev = jnp.where(seq_block < N_CTX, seq_block, 2 * N_CTX - 1 - seq_block)
    upper_half = (seq_block >= N_CTX).astype(jnp.int32)
    source_row = (owner_dev * (2 * CH) + upper_half * CH + seq_pos % CH).astype(jnp.int32)
    device_of = seq_pos // (2 * CH)
    side_of = seq_pos // CH % 2
    target_pos = (jnp.where(side_of == 0, device_of, 2 * N_CTX - 1 - device_of) * CH + seq_pos % CH).astype(jnp.int32)
    query_seq = jnp.take(queries, source_row, axis=0).reshape(row_count, KH, QG, HD)
    grad_seq = jnp.take(grad_out, source_row, axis=0).reshape(row_count, KH, QG, HD)
    key_pad = jnp.concatenate([jnp.zeros((pad_rows, KH * HD), keys.dtype), jnp.take(keys, source_row, axis=0)], axis=0).reshape(row_count + pad_rows, KH, HD)
    value_pad = jnp.concatenate([jnp.zeros((pad_rows, KH * HD), values.dtype), jnp.take(values, source_row, axis=0)], axis=0).reshape(row_count + pad_rows, KH, HD)
    doc_ends = jnp.cumsum(doc_lengths)
    doc_ids = lax.optimization_barrier(jnp.sum((doc_ends[None, :] <= seq_pos[:, None]).astype(jnp.int32), axis=1)).astype(jnp.int32)
    doc_pad = jnp.concatenate([jnp.full((pad_rows,), -1, jnp.int32), doc_ids], axis=0)
    query_offsets = jnp.arange(CH, dtype=jnp.int32)
    key_offsets = jnp.arange(window_rows, dtype=jnp.int32)

    def one_block(totals, block_index):
        key_acc, value_acc = totals
        start_row = (block_index * CH).astype(jnp.int32)
        query_rows = lax.dynamic_slice_in_dim(query_seq, start_row, CH, 0).astype(jnp.float32)
        grad_rows = lax.dynamic_slice_in_dim(grad_seq, start_row, CH, 0).astype(jnp.float32)
        key_window = lax.dynamic_slice_in_dim(key_pad, start_row, window_rows, 0).astype(jnp.float32)
        value_window = lax.dynamic_slice_in_dim(value_pad, start_row, window_rows, 0).astype(jnp.float32)
        query_doc = lax.dynamic_slice_in_dim(doc_ids, start_row, CH, 0)
        key_doc = lax.dynamic_slice_in_dim(doc_pad, start_row, window_rows, 0)
        query_pos = start_row + query_offsets
        key_pos = start_row - pad_rows + key_offsets
        allowed = (key_doc[None, :] == query_doc[:, None]) & (key_pos[None, :] <= query_pos[:, None])
        scores = jnp.einsum('agzd,bgd->gzab', query_rows, key_window) * score_scale
        row_max = lax.optimization_barrier(jnp.max(jnp.where(allowed, scores, MASKED_SCORE), axis=3, keepdims=True))
        exp_terms = jnp.where(allowed, jnp.exp(scores - row_max), 0.0)
        log_total = row_max + jnp.log(lax.optimization_barrier(jnp.sum(exp_terms, axis=3, keepdims=True)))
        prob_full = jnp.where(allowed, jnp.exp(scores - log_total), 0.0)
        prob_low = lax.optimization_barrier(prob_full.astype(jnp.bfloat16)).astype(jnp.float32)
        grad_prob = jnp.einsum('agzd,bgd->gzab', grad_rows, value_window)
        delta_row = lax.optimization_barrier(jnp.sum(prob_full * grad_prob, axis=3, keepdims=True))
        dscore = lax.optimization_barrier((prob_full * (grad_prob - delta_row)).astype(jnp.bfloat16)).astype(jnp.float32)
        query_grad = (score_scale * jnp.einsum('gzab,bgd->agzd', dscore, key_window)).astype(jnp.bfloat16)
        key_part = score_scale * jnp.einsum('gzab,agzd->bgd', dscore, query_rows)
        value_part = jnp.einsum('gzab,agzd->bgd', prob_low, grad_rows)
        key_acc = lax.dynamic_update_slice_in_dim(key_acc, lax.dynamic_slice_in_dim(key_acc, start_row, window_rows, 0) + key_part, start_row, 0)
        value_acc = lax.dynamic_update_slice_in_dim(value_acc, lax.dynamic_slice_in_dim(value_acc, start_row, window_rows, 0) + value_part, start_row, 0)
        return ((key_acc, value_acc), query_grad)
    initial = (jnp.zeros((row_count + pad_rows, KH, HD), jnp.float32), jnp.zeros((row_count + pad_rows, KH, HD), jnp.float32))
    (key_acc, value_acc), query_blocks = lax.scan(one_block, initial, jnp.arange(block_count, dtype=jnp.int32))
    query_grad = jnp.take(query_blocks.reshape(row_count, QH * HD), target_pos, axis=0)
    key_grad = jnp.take(key_acc[pad_rows:].reshape(row_count, KH * HD).astype(jnp.bfloat16), target_pos, axis=0)
    value_grad = jnp.take(value_acc[pad_rows:].reshape(row_count, KH * HD).astype(jnp.bfloat16), target_pos, axis=0)
    return (query_grad, key_grad, value_grad)
```

```python
import math

import jax
import jax.numpy as jnp
from jax import lax
from jax.experimental import pallas as pl
from jax.experimental.pallas import tpu as pltpu
from jax.sharding import PartitionSpec as P

HD = 128
AXES = ("ctx", "kv")
BACK = 8
SLOTS = 12
NEG = -1e30
NT = (((1,), (1,)), ((), ()))
TN = (((0,), (0,)), ((), ()))
SCALE = 1.0 / math.sqrt(HD)
SCALE_LOG2 = math.log2(math.e) / math.sqrt(HD)


def device_of(n_ctx, group, half, part):
    if group < n_ctx // 2:
        return (2 * group + half) * 4 + part
    return (n_ctx - 1 - (2 * (group - n_ctx // 2) + half)) * 4 + part + 2


def pairs(n_ctx, move):
    found = []
    for group in range(n_ctx):
        for half in range(2):
            for part in range(2):
                target = move(group, half, part)
                if 0 <= target[0] < n_ctx:
                    found.append((device_of(n_ctx, group, half, part), device_of(n_ctx, *target)))
    return found


def place():
    n_ctx = lax.axis_size("ctx")
    slot = lax.axis_index("ctx")
    lane = lax.axis_index("kv")
    upper = lane // 2
    block = jnp.where(upper == 0, slot, 2 * n_ctx - 1 - slot)
    return block // 2, block % 2, lane % 2


def kernel(
    lengths_ref, q_ref, g_ref, x_ref, y_refs, dq_ref, keep_ref, send_ref,
    win, acc, s_scr, dp_scr, p_scr, ds_scr, lo_scr, in_sem, out_sem,
):
    step = pl.program_id(0)
    rows = q_ref.shape[0]
    heads = q_ref.shape[1] // HD
    width = (BACK + 1) * rows
    kv_width = win.shape[1] // 2
    group, half, part = place()
    first = 2 * half + part
    sources = (x_ref,) + tuple(y_refs)

    def spot(which, h_rel, y_rel):
        return pl.ds(pl.multiple_of((4 * which + 2 * (half ^ h_rel) + (part ^ y_rel)) * rows, rows), rows)

    def arrivals():
        copies = []
        n = 0
        for which in (2, 1, 0):
            for h_rel in range(2):
                for y_rel in range(2):
                    copies.append(
                        pltpu.make_async_copy(sources[n], win.at[spot(which, h_rel, y_rel)], in_sem.at[n])
                    )
                    n += 1
        return copies

    @pl.when(step == 0)
    def _():
        for copy in arrivals():
            copy.start()
        acc[...] = jnp.zeros_like(acc)
        lens = lengths_ref[...].astype(jnp.float32)
        docs = lens.shape[1]
        below = lax.broadcasted_iota(jnp.int32, (docs, docs), 1) <= lax.broadcasted_iota(
            jnp.int32, (docs, docs), 0
        )
        ends = jnp.sum(jnp.where(below, lens, 0.0), axis=1, keepdims=True)
        start = (4 * group + first) * rows
        pos = (start + lax.broadcasted_iota(jnp.int32, (1, rows), 1)).astype(jnp.float32)
        low = jnp.max(jnp.where(ends <= pos, ends, 0.0), axis=0, keepdims=True).astype(jnp.int32)
        lo_scr[...] = jnp.broadcast_to(low - (start - BACK * rows), lo_scr.shape)
        for copy in arrivals():
            copy.wait()

    lo = lo_scr[0:1, :]
    lo2 = jnp.concatenate([lo, lo], axis=1)
    window = pl.ds(pl.multiple_of(first * rows, rows), width)
    k_cols = pl.ds(pl.multiple_of(step * HD, HD), HD)
    v_cols = pl.ds(pl.multiple_of(kv_width + step * HD, HD), HD)
    keys = win[window, k_cols]
    values = win[window, v_cols]
    column = lax.broadcasted_iota(jnp.int32, (1, 2 * rows), 1) % rows

    def head(ref, index):
        return ref[:, index * HD : (index + 1) * HD]

    for hp in range(heads // 2):
        lanes = slice(hp * 2 * rows, (hp + 1) * 2 * rows)
        q2 = jnp.concatenate([head(q_ref, 2 * hp), head(q_ref, 2 * hp + 1)], axis=0)
        g2 = jnp.concatenate([head(g_ref, 2 * hp), head(g_ref, 2 * hp + 1)], axis=0)
        s_scr[hp] = lax.dot_general(keys, q2, NT, preferred_element_type=jnp.float32)
        dp_scr[hp] = lax.dot_general(values, g2, NT, preferred_element_type=jnp.float32)
        top = jnp.full((8, 2 * rows), NEG, jnp.float32)
        for t in range(BACK + 1):
            here = slice(t * rows, (t + 1) * rows)
            tile = s_scr[hp, here, :]
            key_row = lax.broadcasted_iota(jnp.int32, (rows, 2 * rows), 0) + t * rows
            allowed = key_row >= lo2
            if t == BACK:
                allowed = allowed & (key_row - BACK * rows <= column)
            tile = jnp.where(allowed, tile, NEG)
            s_scr[hp, here, :] = tile
            top = jnp.maximum(top, jnp.max(tile.reshape(rows // 8, 8, 2 * rows), axis=0))
        top = jnp.max(top, axis=0, keepdims=True) * SCALE_LOG2
        total = jnp.zeros((8, 2 * rows), jnp.float32)
        dots = jnp.zeros((8, 2 * rows), jnp.float32)
        for t in range(BACK + 1):
            here = slice(t * rows, (t + 1) * rows)
            weight = jnp.exp2(s_scr[hp, here, :] * SCALE_LOG2 - top)
            s_scr[hp, here, :] = weight
            total = total + jnp.sum(weight.reshape(rows // 8, 8, 2 * rows), axis=0)
            dots = dots + jnp.sum((weight * dp_scr[hp, here, :]).reshape(rows // 8, 8, 2 * rows), axis=0)
        inverse = 1.0 / jnp.sum(total, axis=0, keepdims=True)
        delta = jnp.sum(dots, axis=0, keepdims=True) * inverse
        for t in range(BACK + 1):
            here = slice(t * rows, (t + 1) * rows)
            prob = s_scr[hp, here, :] * inverse
            p_scr[here, lanes] = prob.astype(jnp.bfloat16)
            ds_scr[here, lanes] = (prob * (dp_scr[hp, here, :] - delta)).astype(jnp.bfloat16)
        dq = lax.dot_general(ds_scr[:, lanes], keys, TN, preferred_element_type=jnp.float32) * SCALE
        dq = dq.astype(jnp.bfloat16)
        dq_ref[:, 2 * hp * HD : (2 * hp + 1) * HD] = dq[:rows]
        dq_ref[:, (2 * hp + 1) * HD : (2 * hp + 2) * HD] = dq[rows:]
    q_all = jnp.concatenate([head(q_ref, index) for index in range(heads)], axis=0)
    g_all = jnp.concatenate([head(g_ref, index) for index in range(heads)], axis=0)
    acc[window, v_cols] = jnp.dot(p_scr[...], g_all, preferred_element_type=jnp.float32).astype(jnp.bfloat16)
    acc[window, k_cols] = (jnp.dot(ds_scr[...], q_all, preferred_element_type=jnp.float32) * SCALE).astype(
        jnp.bfloat16
    )

    @pl.when(step == pl.num_programs(0) - 1)
    def _():
        copies = []
        n = 0
        for which in range(3):
            for y_rel in range(2):
                for h_rel, out in ((1, send_ref), (0, keep_ref)):
                    copies.append(
                        pltpu.make_async_copy(
                            acc.at[spot(which, h_rel, y_rel)], out.at[which, y_rel], out_sem.at[n]
                        )
                    )
                    n += 1
        for copy in copies:
            copy.start()
        for copy in copies:
            copy.wait()


def attention(lengths, queries, grad_out, own, arrived):
    rows, q_width = queries.shape
    kv_width = own.shape[1] // 2
    kv_heads = kv_width // HD
    span = q_width // kv_heads
    width = (BACK + 1) * rows
    heads = span // HD
    by_head = pl.BlockSpec((rows, span), lambda i: (0, i))
    anywhere = pl.BlockSpec(memory_space=pl.ANY)
    part = jax.ShapeDtypeStruct((3, 2, rows, 2 * kv_width), jnp.bfloat16)
    return pl.pallas_call(
        kernel,
        grid=(kv_heads,),
        in_specs=[
            pl.BlockSpec(lengths.shape, lambda i: (0, 0)),
            by_head,
            by_head,
            anywhere,
            tuple([anywhere] * len(arrived)),
        ],
        out_specs=[by_head, anywhere, anywhere],
        out_shape=[jax.ShapeDtypeStruct((rows, q_width), jnp.bfloat16), part, part],
        scratch_shapes=[
            pltpu.VMEM((SLOTS * rows, 2 * kv_width), jnp.bfloat16),
            pltpu.VMEM((SLOTS * rows, 2 * kv_width), jnp.bfloat16),
            pltpu.VMEM((heads // 2, width, 2 * rows), jnp.float32),
            pltpu.VMEM((heads // 2, width, 2 * rows), jnp.float32),
            pltpu.VMEM((width, heads * rows), jnp.bfloat16),
            pltpu.VMEM((width, heads * rows), jnp.bfloat16),
            pltpu.VMEM((8, rows), jnp.int32),
            pltpu.SemaphoreType.DMA((SLOTS,)),
            pltpu.SemaphoreType.DMA((SLOTS,)),
        ],
        compiler_params=pltpu.CompilerParams(vmem_limit_bytes=56 * 2**20),
    )(lengths, queries, grad_out, own, tuple(arrived))


def body(queries, keys, values, grad_out, doc_lengths):
    n_ctx = lax.axis_size("ctx")
    swap_part = pairs(n_ctx, lambda g, h, y: (g, h, 1 - y))
    swap_half = pairs(n_ctx, lambda g, h, y: (g, 1 - h, y))

    def ahead(steps):
        return pairs(n_ctx, lambda g, h, y: (g + steps, h, y))

    def sent(value, plan):
        return lax.ppermute(value, AXES, plan)

    def added(*terms):
        return sum(term.astype(jnp.float32) for term in terms)

    own = jnp.concatenate([keys, values], axis=1)
    gathered = []
    for steps in range(3):
        mine = own if steps == 0 else sent(own, ahead(steps))
        other = sent(mine, swap_part)
        gathered += [mine, other, sent(mine, swap_half), sent(other, swap_half)]
    query_grad, keep, send = attention(
        doc_lengths.reshape(1, -1), queries, grad_out, own, gathered[1:]
    )
    got = sent(send, swap_half)
    total = None
    for which in range(3):
        both = added(keep[which], got[which]).astype(jnp.bfloat16)
        summed = added(both[0], sent(both[1], swap_part))
        if which < 2:
            summed = sent(summed.astype(jnp.bfloat16), ahead(which - 2)).astype(jnp.float32)
        total = summed if total is None else total + summed
    total = total.astype(jnp.bfloat16)
    kv_width = keys.shape[1]
    return query_grad, total[:, :kv_width], total[:, kv_width:]


def solution(mesh):
    rows = P(AXES, None)
    return jax.shard_map(
        body,
        mesh=mesh,
        in_specs=(rows, rows, rows, rows, P()),
        out_specs=(rows, rows, rows),
        check_vma=False,
    )
```

```python
import math

import jax
import jax.numpy as jnp
from jax import lax
from jax.experimental import pallas as pl
from jax.experimental.pallas import tpu as pltpu
from jax.sharding import PartitionSpec as P

HD = 128
AXES = ("ctx", "kv")
BACK = 8
NEG = -1e30
NT = (((1,), (1,)), ((), ()))
SCALE = 1.0 / math.sqrt(HD)
SCALE_LOG2 = math.log2(math.e) / math.sqrt(HD)


def device_of(n_ctx, group, core, part):
    if group < n_ctx // 2:
        return (2 * group + core) * 4 + part
    return (2 * (n_ctx - 1 - group) + core) * 4 + part + 2


def pairs(n_ctx, move):
    found = []
    for group in range(n_ctx):
        for core in range(2):
            for part in range(2):
                target = move(group, core, part)
                if 0 <= target[0] < n_ctx:
                    found.append((device_of(n_ctx, group, core, part), device_of(n_ctx, *target)))
    return found


def ahead(n_ctx, steps):
    def move(group, core, part):
        crosses = (group < n_ctx // 2) != (group + steps < n_ctx // 2)
        return group + steps, core, part ^ int(crosses)

    return pairs(n_ctx, move)


def heads_of(ref, cols):
    return ref[:, pl.ds(pl.multiple_of(cols, HD), HD)]


def split_kernel(keys_ref, values_ref, mine_ref, send_ref):
    core = lax.axis_index("ctx") % 2
    kept = mine_ref.shape[1] // (2 * HD)
    for ref, side in ((mine_ref, core), (send_ref, 1 - core)):
        for a in range(kept):
            cols = (side * kept + a) * HD
            ref[:, 2 * a * HD : (2 * a + 1) * HD] = heads_of(keys_ref, cols)
            ref[:, (2 * a + 1) * HD : (2 * a + 2) * HD] = heads_of(values_ref, cols)


def merge_kernel(mine_ref, got_ref, key_ref, value_ref):
    core = lax.axis_index("ctx") % 2
    kept = mine_ref.shape[1] // (2 * HD)
    for ref, side in ((mine_ref, core), (got_ref, 1 - core)):
        for a in range(kept):
            cols = pl.ds(pl.multiple_of((side * kept + a) * HD, HD), HD)
            key_ref[:, cols] = ref[:, 2 * a * HD : (2 * a + 1) * HD]
            value_ref[:, cols] = ref[:, (2 * a + 1) * HD : (2 * a + 2) * HD]


def kernel(
    lengths_ref, q_own_ref, q_got_ref, g_own_ref, g_got_ref, pieces, dq_mine_ref, dq_send_ref, parts,
    win, acc, s_scr, pp_scr, dp_scr, p_scr, ds_scr, q_ref, g_ref, dq_ref,
):
    step = pl.program_id(1)
    rows = q_ref.shape[0]
    heads = q_ref.shape[1] // HD
    width = (BACK + 1) * rows
    n_ctx = lax.axis_size("ctx")
    turn = n_ctx // 2
    slot = lax.axis_index("ctx")
    lane = lax.axis_index("kv")
    upper = lane // 2
    part = lane % 2
    group = jnp.where(upper == 0, slot // 2, n_ctx - 1 - slot // 2)
    mine = (slot % 2) ^ step

    @pl.when(step == 0)
    def _():
        q_ref[...] = q_own_ref[...]
        g_ref[...] = g_own_ref[...]

    @pl.when(step == 1)
    def _():
        q_ref[...] = q_got_ref[...]
        g_ref[...] = g_got_ref[...]

    def spot(which, y_rel, core):
        crossed = jnp.where((group >= turn) & (group < turn + 2 - which), 1, 0)
        index = 4 * which + 2 * (core ^ upper ^ crossed) + (part ^ y_rel ^ crossed)
        return pl.ds(pl.multiple_of(index * rows, rows), rows)

    spots = [(which, y_rel, core) for which in range(3) for y_rel in range(2) for core in range(2)]

    @pl.when(step == 0)
    def _():
        acc[...] = jnp.zeros_like(acc)
        for which, y_rel, core in spots:
            win[spot(which, y_rel, core), :] = pieces[2 * which + y_rel][core * rows : (core + 1) * rows, :]

    first = 2 * (mine ^ upper) + part
    lens = lengths_ref[...].astype(jnp.float32)
    docs = lens.shape[1]
    below = lax.broadcasted_iota(jnp.int32, (docs, docs), 1) <= lax.broadcasted_iota(jnp.int32, (docs, docs), 0)
    ends = jnp.sum(jnp.where(below, lens, 0.0), axis=1, keepdims=True)
    start = (4 * group + first) * rows
    pos = (start + lax.broadcasted_iota(jnp.int32, (1, rows), 1)).astype(jnp.float32)
    lo = jnp.max(jnp.where(ends <= pos, ends, 0.0), axis=0, keepdims=True).astype(jnp.int32)
    lo = lo - (start - BACK * rows)
    lo2 = jnp.concatenate([lo, lo], axis=1)
    base = first * rows
    window = pl.ds(pl.multiple_of(base, rows), width)
    keys_t = win[window, :HD].T
    column = lax.broadcasted_iota(jnp.int32, (1, 2 * rows), 1) % rows

    def key_rows(t):
        return pl.ds(pl.multiple_of(base + t * rows, rows), rows)

    def head(ref, index):
        return ref[:, index * HD : (index + 1) * HD]

    def folded(tile, fold):
        return fold(tile.reshape(rows // 8, 8, 2 * rows), axis=0)

    pair_count = heads // 2
    state = {}

    def pair_of(ref, hp):
        return jnp.concatenate([head(ref, 2 * hp), head(ref, 2 * hp + 1)], axis=0)

    def score_tile(hp, t):
        tile = lax.dot_general(
            win[key_rows(t), :HD], pair_of(q_ref, hp), NT, preferred_element_type=jnp.float32
        )
        key_row = lax.broadcasted_iota(jnp.int32, (rows, 2 * rows), 0) + t * rows
        allowed = key_row >= lo2
        if t == BACK:
            allowed = allowed & (key_row - BACK * rows <= column)
        tile = jnp.where(allowed, tile, NEG)
        s_scr[hp, t * rows : (t + 1) * rows, :] = tile
        peak = folded(tile, jnp.max)
        state["top", hp] = peak if t == 0 else jnp.maximum(state["top", hp], peak)

    def weight_tile(hp, t):
        here = slice(t * rows, (t + 1) * rows)
        if t == 0:
            state["top", hp] = jnp.max(state["top", hp], axis=0, keepdims=True) * SCALE_LOG2
            state["total", hp] = state["dots", hp] = jnp.zeros((8, 2 * rows), jnp.float32)
        weight = jnp.exp2(s_scr[hp, here, :] * SCALE_LOG2 - state["top", hp])
        grad_prob = lax.dot_general(
            win[key_rows(t), HD:], pair_of(g_ref, hp), NT, preferred_element_type=jnp.float32
        )
        pp_scr[hp, here, :] = weight
        dp_scr[hp, here, :] = grad_prob
        state["total", hp] += folded(weight, jnp.sum)
        state["dots", hp] += folded(weight * grad_prob, jnp.sum)

    def prob_tile(hp, t):
        here = slice(t * rows, (t + 1) * rows)
        lanes = slice(hp * 2 * rows, (hp + 1) * 2 * rows)
        if t == 0:
            state["inverse", hp] = 1.0 / jnp.sum(state["total", hp], axis=0, keepdims=True)
            state["delta", hp] = jnp.sum(state["dots", hp], axis=0, keepdims=True) * state["inverse", hp]
        prob = pp_scr[hp, here, :] * state["inverse", hp]
        p_scr[here, lanes] = prob.astype(jnp.bfloat16)
        ds_scr[here, lanes] = (prob * (dp_scr[hp, here, :] - state["delta", hp])).astype(jnp.bfloat16)

    def products(hp):
        lanes = slice(hp * 2 * rows, (hp + 1) * 2 * rows)
        dq = jnp.dot(keys_t, ds_scr[:, lanes], preferred_element_type=jnp.float32).T * SCALE
        dq = dq.astype(jnp.bfloat16)
        dq_ref[:, 2 * hp * HD : (2 * hp + 1) * HD] = dq[:rows]
        dq_ref[:, (2 * hp + 1) * HD : (2 * hp + 2) * HD] = dq[rows:]
        acc[window, :HD] += (
            jnp.dot(ds_scr[:, lanes], pair_of(q_ref, hp), preferred_element_type=jnp.float32) * SCALE
        )
        acc[window, HD:] += jnp.dot(p_scr[:, lanes], pair_of(g_ref, hp), preferred_element_type=jnp.float32)

    for t in range(BACK + 1):
        score_tile(0, t)
    for hp in range(pair_count):
        for t in range(BACK + 1):
            weight_tile(hp, t)
        if hp > 0:
            products(hp - 1)
        for t in range(BACK + 1):
            if hp + 1 < pair_count:
                score_tile(hp + 1, t)
            prob_tile(hp, t)
    products(pair_count - 1)

    @pl.when(step == 0)
    def _():
        dq_mine_ref[...] = dq_ref[...]

    @pl.when(step == 1)
    def _():
        dq_send_ref[...] = dq_ref[...]
        for which, y_rel, core in spots:
            parts[2 * which + y_rel][core * rows : (core + 1) * rows, :] = acc[
                spot(which, y_rel, core), :
            ].astype(jnp.bfloat16)


def attention(lengths, queries, q_got, grad_out, g_got, pieces):
    rows, q_width = q_got.shape
    kv_heads = pieces[0].shape[1] // (2 * HD)
    span = q_width // kv_heads
    heads = span // HD
    width = (BACK + 1) * rows
    by_core = pl.BlockSpec((rows, span), lambda a, r: (0, kv_heads * (lax.axis_index("ctx") % 2) + a))
    by_head = pl.BlockSpec((rows, span), lambda a, r: (0, a))
    piece = pl.BlockSpec((2 * rows, 2 * HD), lambda a, r: (0, a))
    tile = pltpu.VMEM((heads // 2, width, 2 * rows), jnp.float32)
    flat = pltpu.VMEM((width, heads * rows), jnp.bfloat16)
    block = pltpu.VMEM((rows, span), jnp.bfloat16)
    half = jax.ShapeDtypeStruct((rows, q_width), jnp.bfloat16)
    return pl.pallas_call(
        kernel,
        grid=(kv_heads, 2),
        in_specs=[
            pl.BlockSpec(lengths.shape, lambda a, r: (0, 0)),
            by_core,
            by_head,
            by_core,
            by_head,
            [piece] * 6,
        ],
        out_specs=[by_head, by_head, [piece] * 6],
        out_shape=[half, half, [jax.ShapeDtypeStruct(pieces[0].shape, jnp.bfloat16)] * 6],
        scratch_shapes=[
            pltpu.VMEM((12 * rows, 2 * HD), jnp.bfloat16),
            pltpu.VMEM((12 * rows, 2 * HD), jnp.float32),
            tile,
            tile,
            tile,
            flat,
            flat,
            block,
            block,
            block,
        ],
        compiler_params=pltpu.CompilerParams(vmem_limit_bytes=56 * 2**20),
    )(lengths, queries, q_got, grad_out, g_got, pieces)


def body(queries, keys, values, grad_out, doc_lengths):
    n_ctx = lax.axis_size("ctx")
    core = lax.axis_index("ctx") % 2
    swap_part = pairs(n_ctx, lambda g, c, y: (g, c, 1 - y))
    swap_core = pairs(n_ctx, lambda g, c, y: (g, 1 - c, y))
    rows, kv_width = keys.shape

    def sent(value, plan):
        return lax.ppermute(value, AXES, plan)

    def other_heads(value):
        half = value.shape[1] // 2
        return sent(lax.dynamic_slice_in_dim(value, (1 - core) * half, half, 1), swap_core)

    def in_order(mine, got, axis):
        return jnp.where(
            core == 0, jnp.concatenate([mine, got], axis=axis), jnp.concatenate([got, mine], axis=axis)
        )

    def added(*terms):
        return sum(term.astype(jnp.float32) for term in terms)

    chunk = jax.ShapeDtypeStruct(keys.shape, jnp.bfloat16)
    mine, given = pl.pallas_call(split_kernel, out_shape=[chunk, chunk])(keys, values)
    own = in_order(mine, sent(given, swap_core), 0)
    pieces = []
    for which in range(3):
        mine = own if which == 2 else sent(own, ahead(n_ctx, 2 - which))
        pieces += [mine, sent(mine, swap_part)]
    dq_mine, dq_send, parts = attention(
        doc_lengths.reshape(1, -1), queries, other_heads(queries), grad_out, other_heads(grad_out), pieces
    )
    query_grad = in_order(dq_mine, sent(dq_send, swap_core), 1)
    total = None
    for which in range(3):
        summed = added(parts[2 * which], sent(parts[2 * which + 1], swap_part))
        if which < 2:
            summed = sent(summed.astype(jnp.bfloat16), ahead(n_ctx, which - 2)).astype(jnp.float32)
        total = summed if total is None else total + summed
    total = total.astype(jnp.bfloat16)
    given = lax.dynamic_slice_in_dim(total, (1 - core) * rows, rows, 0)
    mine = lax.dynamic_slice_in_dim(total, core * rows, rows, 0)
    key_grad, value_grad = pl.pallas_call(merge_kernel, out_shape=[chunk, chunk])(mine, sent(given, swap_core))
    return query_grad, key_grad, value_grad


def solution(mesh):
    rows = P(AXES, None)
    return jax.shard_map(
        body,
        mesh=mesh,
        in_specs=(rows, rows, rows, rows, P()),
        out_specs=(rows, rows, rows),
        check_vma=False,
    )
```

```python
import math

import jax
import jax.numpy as jnp
from jax import lax
from jax.experimental import pallas as pl
from jax.experimental.pallas import tpu as pltpu
from jax.sharding import PartitionSpec as P

HD = 128
AXES = ("ctx", "kv")
BACK = 8
TILE = 3
NEG = -1e30
NT = (((1,), (1,)), ((), ()))
SCALE = 1.0 / math.sqrt(HD)
SCALE_LOG2 = math.log2(math.e) / math.sqrt(HD)


def device_of(n_ctx, group, core, part):
    if group < n_ctx // 2:
        return (2 * group + core) * 4 + part
    return (2 * (n_ctx - 1 - group) + core) * 4 + part + 2


def pairs(n_ctx, move):
    found = []
    for group in range(n_ctx):
        for core in range(2):
            for part in range(2):
                target = move(group, core, part)
                if 0 <= target[0] < n_ctx:
                    found.append((device_of(n_ctx, group, core, part), device_of(n_ctx, *target)))
    return found


def ahead(n_ctx, steps):
    def move(group, core, part):
        crosses = (group < n_ctx // 2) != (group + steps < n_ctx // 2)
        return group + steps, core, part ^ int(crosses)

    return pairs(n_ctx, move)


def heads_of(ref, cols):
    return ref[:, pl.ds(pl.multiple_of(cols, HD), HD)]


def split_kernel(keys_ref, values_ref, mine_ref, send_ref):
    core = lax.axis_index("ctx") % 2
    kept = mine_ref.shape[1] // (2 * HD)
    for ref, side in ((mine_ref, core), (send_ref, 1 - core)):
        for a in range(kept):
            cols = (side * kept + a) * HD
            ref[:, 2 * a * HD : (2 * a + 1) * HD] = heads_of(keys_ref, cols)
            ref[:, (2 * a + 1) * HD : (2 * a + 2) * HD] = heads_of(values_ref, cols)


def merge_kernel(mine_ref, got_ref, key_ref, value_ref):
    core = lax.axis_index("ctx") % 2
    kept = mine_ref.shape[1] // (2 * HD)
    for ref, side in ((mine_ref, core), (got_ref, 1 - core)):
        for a in range(kept):
            cols = pl.ds(pl.multiple_of((side * kept + a) * HD, HD), HD)
            key_ref[:, cols] = ref[:, 2 * a * HD : (2 * a + 1) * HD]
            value_ref[:, cols] = ref[:, (2 * a + 1) * HD : (2 * a + 2) * HD]


def kernel(
    lengths_ref, q_own_ref, q_got_ref, g_own_ref, g_got_ref, pieces, dq_mine_ref, dq_send_ref, parts,
    win, acc, key_acc, value_acc, s_scr, pp_scr, dp_scr, p_scr, ds_scr,
):
    q_refs, g_refs, dq_refs = (q_own_ref, q_got_ref), (g_own_ref, g_got_ref), (dq_mine_ref, dq_send_ref)
    rows, span = q_own_ref.shape
    pair_count = span // (2 * HD)
    width = (BACK + 1) * rows
    high = TILE * rows
    n_ctx = lax.axis_size("ctx")
    turn = n_ctx // 2
    slot = lax.axis_index("ctx")
    lane = lax.axis_index("kv")
    upper = lane // 2
    part = lane % 2
    core = slot % 2
    group = jnp.where(upper == 0, slot // 2, n_ctx - 1 - slot // 2)

    def spot(which, y_rel, core):
        crossed = jnp.where((group >= turn) & (group < turn + 2 - which), 1, 0)
        index = 4 * which + 2 * (core ^ upper ^ crossed) + (part ^ y_rel ^ crossed)
        return pl.ds(pl.multiple_of(index * rows, rows), rows)

    spots = [(which, y_rel, core) for which in range(3) for y_rel in range(2) for core in range(2)]
    for which, y_rel, side in spots:
        win[spot(which, y_rel, side), :] = pieces[2 * which + y_rel][side * rows : (side + 1) * rows, :]

    lens = lengths_ref[...].astype(jnp.float32)
    docs = lens.shape[1]
    below = lax.broadcasted_iota(jnp.int32, (docs, docs), 1) <= lax.broadcasted_iota(jnp.int32, (docs, docs), 0)
    ends = jnp.sum(jnp.where(below, lens, 0.0), axis=1, keepdims=True)
    column = lax.broadcasted_iota(jnp.int32, (1, 2 * rows), 1) % rows
    base, low, keys_t = [], [], []
    for other in range(2):
        first = 2 * (core ^ other ^ upper) + part
        start = (4 * group + first) * rows
        pos = (start + lax.broadcasted_iota(jnp.int32, (1, rows), 1)).astype(jnp.float32)
        lo = jnp.max(jnp.where(ends <= pos, ends, 0.0), axis=0, keepdims=True).astype(jnp.int32)
        lo = lo - (start - BACK * rows)
        low.append(jnp.concatenate([lo, lo], axis=1))
        base.append(first * rows)
        keys_t.append(win[pl.ds(pl.multiple_of(first * rows, rows), width), :HD].T)

    units = [(other, pair) for other in range(2) for pair in range(pair_count)]
    tiles = range((BACK + 1) // TILE)
    state = {}

    def key_rows(unit, t):
        return pl.ds(pl.multiple_of(base[units[unit][0]] + t * high, rows), high)

    def lanes(unit):
        return slice(unit * 2 * rows, (unit + 1) * 2 * rows)

    def pair_of(refs, unit):
        other, pair = units[unit]
        return jnp.concatenate(
            [refs[other][:, (2 * pair + i) * HD : (2 * pair + i + 1) * HD] for i in range(2)], axis=0
        )

    def folded(tile, fold):
        return fold(tile.reshape(high // 8, 8, 2 * rows), axis=0)

    def scores(unit):
        slot = unit % 4
        for t in tiles:
            tile = lax.dot_general(
                win[key_rows(unit, t), :HD], pair_of(q_refs, unit), NT, preferred_element_type=jnp.float32
            )
            key_row = lax.broadcasted_iota(jnp.int32, (high, 2 * rows), 0) + t * high
            allowed = key_row >= low[units[unit][0]]
            if t == tiles[-1]:
                allowed = allowed & (key_row - BACK * rows <= column)
            tile = jnp.where(allowed, tile, NEG)
            s_scr[slot, t * high : (t + 1) * high, :] = tile
            peak = folded(tile, jnp.max)
            state["top", unit] = peak if t == 0 else jnp.maximum(state["top", unit], peak)
        state["top", unit] = jnp.max(state["top", unit], axis=0, keepdims=True) * SCALE_LOG2
        state["total", unit] = state["dots", unit] = jnp.zeros((8, 2 * rows), jnp.float32)

    def weight_tile(unit, t):
        here = slice(t * high, (t + 1) * high)
        weight = jnp.exp2(s_scr[unit % 4, here, :] * SCALE_LOG2 - state["top", unit])
        grad_prob = lax.dot_general(
            win[key_rows(unit, t), HD:], pair_of(g_refs, unit), NT, preferred_element_type=jnp.float32
        )
        pp_scr[unit % 4, here, :] = weight
        dp_scr[unit % 4, here, :] = grad_prob
        state["total", unit] += folded(weight, jnp.sum)
        state["dots", unit] += folded(weight * grad_prob, jnp.sum)

    def sums(unit):
        state["inverse", unit] = 1.0 / jnp.sum(state["total", unit], axis=0, keepdims=True)
        state["delta", unit] = jnp.sum(state["dots", unit], axis=0, keepdims=True) * state["inverse", unit]

    def prob_tile(unit, t):
        here = slice(t * high, (t + 1) * high)
        prob = pp_scr[unit % 4, here, :] * state["inverse", unit]
        p_scr[here, lanes(unit % 4)] = prob.astype(jnp.bfloat16)
        ds_scr[here, lanes(unit % 4)] = (prob * (dp_scr[unit % 4, here, :] - state["delta", unit])).astype(
            jnp.bfloat16
        )

    def products(unit):
        other, pair = units[unit]
        dscore, prob = ds_scr[:, lanes(unit % 4)], p_scr[:, lanes(unit % 4)]
        dq = jnp.dot(keys_t[other], dscore, preferred_element_type=jnp.float32).T * SCALE
        dq = dq.astype(jnp.bfloat16)
        dq_refs[other][:, 2 * pair * HD : (2 * pair + 1) * HD] = dq[:rows]
        dq_refs[other][:, (2 * pair + 1) * HD : (2 * pair + 2) * HD] = dq[rows:]
        key_part = jnp.dot(dscore, pair_of(q_refs, unit), preferred_element_type=jnp.float32)
        value_part = jnp.dot(prob, pair_of(g_refs, unit), preferred_element_type=jnp.float32)
        if pair == 0:
            key_acc[other] = key_part
            value_acc[other] = value_part
        else:
            key_acc[other] += key_part
            value_acc[other] += value_part

    scores(0)
    for t in tiles:
        weight_tile(0, t)
    sums(0)
    scores(1)
    for unit in range(len(units)):
        for t in tiles:
            prob_tile(unit, t)
            if unit + 1 < len(units):
                weight_tile(unit + 1, t)
        if unit + 1 < len(units):
            sums(unit + 1)
        if unit + 2 < len(units):
            scores(unit + 2)
        products(unit)

    acc[...] = jnp.zeros_like(acc)
    for other in range(2):
        here = pl.ds(pl.multiple_of(base[other], rows), width)
        acc[here, :HD] += key_acc[other] * SCALE
        acc[here, HD:] += value_acc[other]
    for which, y_rel, side in spots:
        parts[2 * which + y_rel][side * rows : (side + 1) * rows, :] = acc[spot(which, y_rel, side), :].astype(
            jnp.bfloat16
        )


def attention(lengths, queries, q_got, grad_out, g_got, pieces):
    rows, q_width = q_got.shape
    kv_heads = pieces[0].shape[1] // (2 * HD)
    span = q_width // kv_heads
    heads = span // HD
    width = (BACK + 1) * rows
    by_core = pl.BlockSpec((rows, span), lambda a: (0, kv_heads * (lax.axis_index("ctx") % 2) + a))
    by_head = pl.BlockSpec((rows, span), lambda a: (0, a))
    piece = pl.BlockSpec((2 * rows, 2 * HD), lambda a: (0, a))
    tile = pltpu.VMEM((heads // 2, width, 2 * rows), jnp.float32)
    flat = pltpu.VMEM((width, heads * rows), jnp.bfloat16)
    half = jax.ShapeDtypeStruct((rows, q_width), jnp.bfloat16)
    return pl.pallas_call(
        kernel,
        grid=(kv_heads,),
        in_specs=[
            pl.BlockSpec(lengths.shape, lambda a: (0, 0)),
            by_core,
            by_head,
            by_core,
            by_head,
            [piece] * 6,
        ],
        out_specs=[by_head, by_head, [piece] * 6],
        out_shape=[half, half, [jax.ShapeDtypeStruct(pieces[0].shape, jnp.bfloat16)] * 6],
        scratch_shapes=[
            pltpu.VMEM((12 * rows, 2 * HD), jnp.bfloat16),
            pltpu.VMEM((12 * rows, 2 * HD), jnp.float32),
            pltpu.VMEM((2, width, HD), jnp.float32),
            pltpu.VMEM((2, width, HD), jnp.float32),
            tile,
            tile,
            tile,
            flat,
            flat,
        ],
        compiler_params=pltpu.CompilerParams(vmem_limit_bytes=56 * 2**20),
    )(lengths, queries, q_got, grad_out, g_got, pieces)


def body(queries, keys, values, grad_out, doc_lengths):
    n_ctx = lax.axis_size("ctx")
    core = lax.axis_index("ctx") % 2
    swap_part = pairs(n_ctx, lambda g, c, y: (g, c, 1 - y))
    swap_core = pairs(n_ctx, lambda g, c, y: (g, 1 - c, y))
    rows, kv_width = keys.shape

    def sent(value, plan):
        return lax.ppermute(value, AXES, plan)

    def other_heads(value):
        half = value.shape[1] // 2
        return sent(lax.dynamic_slice_in_dim(value, (1 - core) * half, half, 1), swap_core)

    def in_order(mine, got, axis):
        return jnp.where(
            core == 0, jnp.concatenate([mine, got], axis=axis), jnp.concatenate([got, mine], axis=axis)
        )

    def added(*terms):
        return sum(term.astype(jnp.float32) for term in terms)

    chunk = jax.ShapeDtypeStruct(keys.shape, jnp.bfloat16)
    mine, given = pl.pallas_call(split_kernel, out_shape=[chunk, chunk])(keys, values)
    own = in_order(mine, sent(given, swap_core), 0)
    far, near, beside = sent(own, ahead(n_ctx, 2)), sent(own, ahead(n_ctx, 1)), sent(own, swap_part)
    near, beside = lax.optimization_barrier((near, beside))
    pieces = [far, sent(far, swap_part), near, sent(near, swap_part), own, beside]
    dq_mine, dq_send, parts = attention(
        doc_lengths.reshape(1, -1), queries, other_heads(queries), grad_out, other_heads(grad_out), pieces
    )
    query_grad = in_order(dq_mine, sent(dq_send, swap_core), 1)
    total = None
    for which in range(3):
        summed = added(parts[2 * which], sent(parts[2 * which + 1], swap_part))
        if which < 2:
            summed = sent(summed.astype(jnp.bfloat16), ahead(n_ctx, which - 2))
            summed = summed.astype(jnp.float32)
        total = summed if total is None else total + summed
    total = total.astype(jnp.bfloat16)
    given = lax.dynamic_slice_in_dim(total, (1 - core) * rows, rows, 0)
    mine = lax.dynamic_slice_in_dim(total, core * rows, rows, 0)
    key_grad, value_grad = pl.pallas_call(merge_kernel, out_shape=[chunk, chunk])(mine, sent(given, swap_core))
    return query_grad, key_grad, value_grad


def solution(mesh):
    rows = P(AXES, None)
    return jax.shard_map(
        body,
        mesh=mesh,
        in_specs=(rows, rows, rows, rows, P()),
        out_specs=(rows, rows, rows),
        check_vma=False,
    )
```

```python
import math

import jax
import jax.numpy as jnp
from jax import lax
from jax.experimental import pallas as pl
from jax.experimental.pallas import tpu as pltpu
from jax.sharding import PartitionSpec as P

HD = 128
AXES = ("ctx", "kv")
BACK = 8
TILE = 3
NEG = -1e30
NT = (((1,), (1,)), ((), ()))
SCALE = 1.0 / math.sqrt(HD)
SCALE_LOG2 = math.log2(math.e) / math.sqrt(HD)


def device_of(n_ctx, group, core, part):
    if group < n_ctx // 2:
        return (2 * group + core) * 4 + part
    return (2 * (n_ctx - 1 - group) + core) * 4 + part + 2


def pairs(n_ctx, move):
    found = []
    for group in range(n_ctx):
        for core in range(2):
            for part in range(2):
                target = move(group, core, part)
                if 0 <= target[0] < n_ctx:
                    found.append((device_of(n_ctx, group, core, part), device_of(n_ctx, *target)))
    return found


def ahead(n_ctx, steps):
    def move(group, core, part):
        crosses = (group < n_ctx // 2) != (group + steps < n_ctx // 2)
        return group + steps, core, part ^ int(crosses)

    return pairs(n_ctx, move)


def heads_of(ref, cols):
    return ref[:, pl.ds(pl.multiple_of(cols, HD), HD)]


def split_kernel(keys_ref, values_ref, mine_ref, send_ref):
    core = lax.axis_index("ctx") % 2
    kept = mine_ref.shape[1] // (2 * HD)
    for ref, side in ((mine_ref, core), (send_ref, 1 - core)):
        for a in range(kept):
            cols = (side * kept + a) * HD
            ref[:, 2 * a * HD : (2 * a + 1) * HD] = heads_of(keys_ref, cols)
            ref[:, (2 * a + 1) * HD : (2 * a + 2) * HD] = heads_of(values_ref, cols)


def merge_kernel(mine_ref, got_ref, key_ref, value_ref):
    core = lax.axis_index("ctx") % 2
    kept = mine_ref.shape[1] // (2 * HD)
    for ref, side in ((mine_ref, core), (got_ref, 1 - core)):
        for a in range(kept):
            cols = pl.ds(pl.multiple_of((side * kept + a) * HD, HD), HD)
            key_ref[:, cols] = ref[:, 2 * a * HD : (2 * a + 1) * HD]
            value_ref[:, cols] = ref[:, (2 * a + 1) * HD : (2 * a + 2) * HD]


def kernel(
    lengths_ref, q_own_ref, q_got_ref, g_own_ref, g_got_ref, pieces, dq_mine_ref, dq_send_ref, parts,
    win, acc, key_acc, value_acc, s_scr, pp_scr, dp_scr, p_scr, ds_scr,
):
    q_refs, g_refs, dq_refs = (q_own_ref, q_got_ref), (g_own_ref, g_got_ref), (dq_mine_ref, dq_send_ref)
    rows, span = q_own_ref.shape
    pair_count = span // (2 * HD)
    width = (BACK + 1) * rows
    high = TILE * rows
    n_ctx = lax.axis_size("ctx")
    turn = n_ctx // 2
    slot = lax.axis_index("ctx")
    lane = lax.axis_index("kv")
    upper = lane // 2
    part = lane % 2
    core = slot % 2
    group = jnp.where(upper == 0, slot // 2, n_ctx - 1 - slot // 2)

    def spot(which, y_rel, core):
        crossed = jnp.where((group >= turn) & (group < turn + 2 - which), 1, 0)
        index = 4 * which + 2 * (core ^ upper ^ crossed) + (part ^ y_rel ^ crossed)
        return pl.ds(pl.multiple_of(index * rows, rows), rows)

    spots = [(which, y_rel, core) for which in range(3) for y_rel in range(2) for core in range(2)]
    for which, y_rel, side in spots:
        win[spot(which, y_rel, side), :] = pieces[2 * which + y_rel][side * rows : (side + 1) * rows, :]

    lens = lengths_ref[...].astype(jnp.float32)
    docs = lens.shape[1]
    below = lax.broadcasted_iota(jnp.int32, (docs, docs), 1) <= lax.broadcasted_iota(jnp.int32, (docs, docs), 0)
    ends = jnp.sum(jnp.where(below, lens, 0.0), axis=1, keepdims=True)
    column = lax.broadcasted_iota(jnp.int32, (1, 2 * rows), 1) % rows
    base, low, keys_t = [], [], []
    for other in range(2):
        first = 2 * (core ^ other ^ upper) + part
        start = (4 * group + first) * rows
        pos = (start + lax.broadcasted_iota(jnp.int32, (1, rows), 1)).astype(jnp.float32)
        lo = jnp.max(jnp.where(ends <= pos, ends, 0.0), axis=0, keepdims=True).astype(jnp.int32)
        lo = lo - (start - BACK * rows)
        low.append(jnp.concatenate([lo, lo], axis=1))
        base.append(first * rows)
        keys_t.append(win[pl.ds(pl.multiple_of(first * rows, rows), width), :HD].T)

    units = [(other, pair) for other in range(2) for pair in range(pair_count)]
    tiles = range((BACK + 1) // TILE)
    state = {}

    def key_rows(unit, t):
        return pl.ds(pl.multiple_of(base[units[unit][0]] + t * high, rows), high)

    def lanes(unit):
        return slice(unit * 2 * rows, (unit + 1) * 2 * rows)

    def pair_of(refs, unit):
        other, pair = units[unit]
        return jnp.concatenate(
            [refs[other][:, (2 * pair + i) * HD : (2 * pair + i + 1) * HD] for i in range(2)], axis=0
        )

    def folded(tile, fold):
        return fold(tile.reshape(high // 8, 8, 2 * rows), axis=0)

    def scores(unit):
        slot = unit % 4
        for t in tiles:
            tile = lax.dot_general(
                win[key_rows(unit, t), :HD], pair_of(q_refs, unit), NT, preferred_element_type=jnp.float32
            )
            key_row = lax.broadcasted_iota(jnp.int32, (high, 2 * rows), 0) + t * high
            allowed = key_row >= low[units[unit][0]]
            if t == tiles[-1]:
                allowed = allowed & (key_row - BACK * rows <= column)
            tile = jnp.where(allowed, tile, NEG)
            s_scr[slot, t * high : (t + 1) * high, :] = tile
            peak = folded(tile, jnp.max)
            state["top", unit] = peak if t == 0 else jnp.maximum(state["top", unit], peak)
        state["top", unit] = jnp.max(state["top", unit], axis=0, keepdims=True) * SCALE_LOG2
        state["total", unit] = state["dots", unit] = jnp.zeros((8, 2 * rows), jnp.float32)

    def weight_tile(unit, t):
        here = slice(t * high, (t + 1) * high)
        weight = jnp.exp2(s_scr[unit % 4, here, :] * SCALE_LOG2 - state["top", unit])
        grad_prob = lax.dot_general(
            win[key_rows(unit, t), HD:], pair_of(g_refs, unit), NT, preferred_element_type=jnp.float32
        )
        pp_scr[unit % 4, here, :] = weight
        dp_scr[unit % 4, here, :] = grad_prob
        state["total", unit] += folded(weight, jnp.sum)
        state["dots", unit] += folded(weight * grad_prob, jnp.sum)

    def sums(unit):
        state["inverse", unit] = 1.0 / jnp.sum(state["total", unit], axis=0, keepdims=True)
        state["delta", unit] = jnp.sum(state["dots", unit], axis=0, keepdims=True) * state["inverse", unit]

    def prob_tile(unit, t):
        here = slice(t * high, (t + 1) * high)
        prob = pp_scr[unit % 4, here, :] * state["inverse", unit]
        p_scr[here, lanes(unit % 4)] = prob.astype(jnp.bfloat16)
        ds_scr[here, lanes(unit % 4)] = (prob * (dp_scr[unit % 4, here, :] - state["delta", unit])).astype(
            jnp.bfloat16
        )

    def products(unit):
        other, pair = units[unit]
        dscore, prob = ds_scr[:, lanes(unit % 4)], p_scr[:, lanes(unit % 4)]
        dq = jnp.dot(keys_t[other], dscore, preferred_element_type=jnp.float32).T * SCALE
        dq = dq.astype(jnp.bfloat16)
        dq_refs[other][:, 2 * pair * HD : (2 * pair + 1) * HD] = dq[:rows]
        dq_refs[other][:, (2 * pair + 1) * HD : (2 * pair + 2) * HD] = dq[rows:]
        key_part = jnp.dot(dscore, pair_of(q_refs, unit), preferred_element_type=jnp.float32)
        value_part = jnp.dot(prob, pair_of(g_refs, unit), preferred_element_type=jnp.float32)
        if pair == 0:
            key_acc[other] = key_part
            value_acc[other] = value_part
        else:
            key_acc[other] += key_part
            value_acc[other] += value_part

    scores(0)
    for t in tiles:
        weight_tile(0, t)
    sums(0)
    scores(1)
    for unit in range(len(units)):
        for t in tiles:
            prob_tile(unit, t)
            if unit + 1 < len(units):
                weight_tile(unit + 1, t)
        if unit + 1 < len(units):
            sums(unit + 1)
        if unit + 2 < len(units):
            scores(unit + 2)
        products(unit)

    acc[...] = jnp.zeros_like(acc)
    for other in range(2):
        here = pl.ds(pl.multiple_of(base[other], rows), width)
        acc[here, :HD] += key_acc[other] * SCALE
        acc[here, HD:] += value_acc[other]
    for which, y_rel, side in spots:
        parts[2 * which + y_rel][side * rows : (side + 1) * rows, :] = acc[spot(which, y_rel, side), :].astype(
            jnp.bfloat16
        )


def attention(lengths, queries, q_got, grad_out, g_got, pieces):
    rows, q_width = q_got.shape
    kv_heads = pieces[0].shape[1] // (2 * HD)
    span = q_width // kv_heads
    heads = span // HD
    width = (BACK + 1) * rows
    by_core = pl.BlockSpec((rows, span), lambda a: (0, kv_heads * (lax.axis_index("ctx") % 2) + a))
    by_head = pl.BlockSpec((rows, span), lambda a: (0, a))
    piece = pl.BlockSpec((2 * rows, 2 * HD), lambda a: (0, a))
    tile = pltpu.VMEM((heads // 2, width, 2 * rows), jnp.float32)
    flat = pltpu.VMEM((width, heads * rows), jnp.bfloat16)
    half = jax.ShapeDtypeStruct((rows, q_width), jnp.bfloat16)
    return pl.pallas_call(
        kernel,
        grid=(kv_heads,),
        in_specs=[
            pl.BlockSpec(lengths.shape, lambda a: (0, 0)),
            by_core,
            by_head,
            by_core,
            by_head,
            [piece] * 6,
        ],
        out_specs=[by_head, by_head, [piece] * 6],
        out_shape=[half, half, [jax.ShapeDtypeStruct(pieces[0].shape, jnp.bfloat16)] * 6],
        scratch_shapes=[
            pltpu.VMEM((12 * rows, 2 * HD), jnp.bfloat16),
            pltpu.VMEM((12 * rows, 2 * HD), jnp.float32),
            pltpu.VMEM((2, width, HD), jnp.float32),
            pltpu.VMEM((2, width, HD), jnp.float32),
            tile,
            tile,
            tile,
            flat,
            flat,
        ],
        compiler_params=pltpu.CompilerParams(vmem_limit_bytes=36 * 2**20),
    )(lengths, queries, q_got, grad_out, g_got, pieces)


def body(queries, keys, values, grad_out, doc_lengths):
    n_ctx = lax.axis_size("ctx")
    core = lax.axis_index("ctx") % 2
    swap_part = pairs(n_ctx, lambda g, c, y: (g, c, 1 - y))
    swap_core = pairs(n_ctx, lambda g, c, y: (g, 1 - c, y))
    rows, kv_width = keys.shape

    def sent(value, plan):
        return lax.ppermute(value, AXES, plan)

    def other_heads(value):
        half = value.shape[1] // 2
        return sent(lax.dynamic_slice_in_dim(value, (1 - core) * half, half, 1), swap_core)

    def in_order(mine, got, axis):
        return jnp.where(
            core == 0, jnp.concatenate([mine, got], axis=axis), jnp.concatenate([got, mine], axis=axis)
        )

    def added(*terms):
        return sum(term.astype(jnp.float32) for term in terms)

    chunk = jax.ShapeDtypeStruct(keys.shape, jnp.bfloat16)
    small = pltpu.CompilerParams(vmem_limit_bytes=4 * 2**20)
    mine, given = pl.pallas_call(split_kernel, out_shape=[chunk, chunk], compiler_params=small)(keys, values)
    own = in_order(mine, sent(given, swap_core), 0)
    far, near, beside = sent(own, ahead(n_ctx, 2)), sent(own, ahead(n_ctx, 1)), sent(own, swap_part)
    near, beside = lax.optimization_barrier((near, beside))
    pieces = [far, sent(far, swap_part), near, sent(near, swap_part), own, beside]
    dq_mine, dq_send, parts = attention(
        doc_lengths.reshape(1, -1), queries, other_heads(queries), grad_out, other_heads(grad_out), pieces
    )
    query_grad = in_order(dq_mine, sent(dq_send, swap_core), 1)
    total = None
    for which in range(3):
        summed = added(parts[2 * which], sent(parts[2 * which + 1], swap_part))
        if which < 2:
            summed = sent(summed.astype(jnp.bfloat16), ahead(n_ctx, which - 2))
            summed = summed.astype(jnp.float32)
        total = summed if total is None else total + summed
    total = total.astype(jnp.bfloat16)
    given = lax.dynamic_slice_in_dim(total, (1 - core) * rows, rows, 0)
    mine = lax.dynamic_slice_in_dim(total, core * rows, rows, 0)
    key_grad, value_grad = pl.pallas_call(merge_kernel, out_shape=[chunk, chunk], compiler_params=small)(mine, sent(given, swap_core))
    return query_grad, key_grad, value_grad


def solution(mesh):
    rows = P(AXES, None)
    return jax.shard_map(
        body,
        mesh=mesh,
        in_specs=(rows, rows, rows, rows, P()),
        out_specs=(rows, rows, rows),
        check_vma=False,
    )
```

```python
import math

import jax
import jax.numpy as jnp
from jax import lax
from jax.experimental import pallas as pl
from jax.experimental.pallas import tpu as pltpu
from jax.sharding import PartitionSpec as P

HD = 128
AXES = ("ctx", "kv")
BACK = 8
TILE = 3
NEG = -1e30
NT = (((1,), (1,)), ((), ()))
SCALE = 1.0 / math.sqrt(HD)
SCALE_LOG2 = math.log2(math.e) / math.sqrt(HD)


def device_of(n_ctx, group, core, part):
    if group < n_ctx // 2:
        return (2 * group + core) * 4 + part
    return (2 * (n_ctx - 1 - group) + core) * 4 + part + 2


def pairs(n_ctx, move):
    found = []
    for group in range(n_ctx):
        for core in range(2):
            for part in range(2):
                target = move(group, core, part)
                if 0 <= target[0] < n_ctx:
                    found.append((device_of(n_ctx, group, core, part), device_of(n_ctx, *target)))
    return found


def ahead(n_ctx, steps):
    def move(group, core, part):
        crosses = (group < n_ctx // 2) != (group + steps < n_ctx // 2)
        return group + steps, core, part ^ int(crosses)

    return pairs(n_ctx, move)


def heads_of(ref, cols):
    return ref[:, pl.ds(pl.multiple_of(cols, HD), HD)]


def split_kernel(keys_ref, values_ref, mine_ref, send_ref):
    core = lax.axis_index("ctx") % 2
    kept = mine_ref.shape[1] // (2 * HD)
    for ref, side in ((mine_ref, core), (send_ref, 1 - core)):
        for a in range(kept):
            cols = (side * kept + a) * HD
            ref[:, 2 * a * HD : (2 * a + 1) * HD] = heads_of(keys_ref, cols)
            ref[:, (2 * a + 1) * HD : (2 * a + 2) * HD] = heads_of(values_ref, cols)


def merge_kernel(mine_ref, got_ref, key_ref, value_ref):
    core = lax.axis_index("ctx") % 2
    kept = mine_ref.shape[1] // (2 * HD)
    for ref, side in ((mine_ref, core), (got_ref, 1 - core)):
        for a in range(kept):
            cols = pl.ds(pl.multiple_of((side * kept + a) * HD, HD), HD)
            key_ref[:, cols] = ref[:, 2 * a * HD : (2 * a + 1) * HD]
            value_ref[:, cols] = ref[:, (2 * a + 1) * HD : (2 * a + 2) * HD]


def kernel(
    lengths_ref, q_own_ref, q_got_ref, g_own_ref, g_got_ref, pieces, dq_mine_ref, dq_send_ref, parts,
    win, acc, key_acc, value_acc, s_scr, pp_scr, dp_scr, p_scr, ds_scr,
):
    q_refs, g_refs, dq_refs = (q_own_ref, q_got_ref), (g_own_ref, g_got_ref), (dq_mine_ref, dq_send_ref)
    rows, span = q_own_ref.shape
    pair_count = span // (2 * HD)
    width = (BACK + 1) * rows
    high = TILE * rows
    n_ctx = lax.axis_size("ctx")
    turn = n_ctx // 2
    slot = lax.axis_index("ctx")
    lane = lax.axis_index("kv")
    upper = lane // 2
    part = lane % 2
    core = slot % 2
    group = jnp.where(upper == 0, slot // 2, n_ctx - 1 - slot // 2)

    def spot(which, y_rel, core):
        crossed = jnp.where((group >= turn) & (group < turn + 2 - which), 1, 0)
        index = 4 * which + 2 * (core ^ upper ^ crossed) + (part ^ y_rel ^ crossed)
        return pl.ds(pl.multiple_of(index * rows, rows), rows)

    spots = [(which, y_rel, core) for which in range(3) for y_rel in range(2) for core in range(2)]
    for which, y_rel, side in spots:
        win[spot(which, y_rel, side), :] = pieces[2 * which + y_rel][side * rows : (side + 1) * rows, :]

    lens = lengths_ref[...].astype(jnp.float32)
    docs = lens.shape[1]
    below = lax.broadcasted_iota(jnp.int32, (docs, docs), 1) <= lax.broadcasted_iota(jnp.int32, (docs, docs), 0)
    ends = jnp.sum(jnp.where(below, lens, 0.0), axis=1, keepdims=True)
    column = lax.broadcasted_iota(jnp.int32, (1, 2 * rows), 1) % rows
    base, low, keys_t = [], [], []
    for other in range(2):
        first = 2 * (core ^ other ^ upper) + part
        start = (4 * group + first) * rows
        pos = (start + lax.broadcasted_iota(jnp.int32, (1, rows), 1)).astype(jnp.float32)
        lo = jnp.max(jnp.where(ends <= pos, ends, 0.0), axis=0, keepdims=True).astype(jnp.int32)
        lo = lo - (start - BACK * rows)
        low.append(jnp.concatenate([lo, lo], axis=1))
        base.append(first * rows)
        keys_t.append(win[pl.ds(pl.multiple_of(first * rows, rows), width), :HD].T)

    units = [(other, pair) for other in range(2) for pair in range(pair_count)]
    tiles = range((BACK + 1) // TILE)
    state = {}

    def key_rows(unit, t):
        return pl.ds(pl.multiple_of(base[units[unit][0]] + t * high, rows), high)

    def lanes(unit):
        return slice(unit * 2 * rows, (unit + 1) * 2 * rows)

    def pair_of(refs, unit):
        other, pair = units[unit]
        return jnp.concatenate(
            [refs[other][:, (2 * pair + i) * HD : (2 * pair + i + 1) * HD] for i in range(2)], axis=0
        )

    def folded(tile, fold):
        return fold(tile.reshape(high // 8, 8, 2 * rows), axis=0)

    def scores(unit):
        slot = unit % 4
        for t in tiles:
            tile = lax.dot_general(
                win[key_rows(unit, t), :HD], pair_of(q_refs, unit), NT, preferred_element_type=jnp.float32
            )
            key_row = lax.broadcasted_iota(jnp.int32, (high, 2 * rows), 0) + t * high
            allowed = key_row >= low[units[unit][0]]
            if t == tiles[-1]:
                allowed = allowed & (key_row - BACK * rows <= column)
            tile = jnp.where(allowed, tile, NEG)
            s_scr[slot, t * high : (t + 1) * high, :] = tile
            peak = folded(tile, jnp.max)
            state["top", unit] = peak if t == 0 else jnp.maximum(state["top", unit], peak)
        state["top", unit] = jnp.max(state["top", unit], axis=0, keepdims=True) * SCALE_LOG2
        state["total", unit] = state["dots", unit] = jnp.zeros((8, 2 * rows), jnp.float32)

    def weight_tile(unit, t):
        here = slice(t * high, (t + 1) * high)
        weight = jnp.exp2(s_scr[unit % 4, here, :] * SCALE_LOG2 - state["top", unit])
        grad_prob = lax.dot_general(
            win[key_rows(unit, t), HD:], pair_of(g_refs, unit), NT, preferred_element_type=jnp.float32
        )
        pp_scr[unit % 4, here, :] = weight
        dp_scr[unit % 4, here, :] = grad_prob
        state["total", unit] += folded(weight, jnp.sum)
        state["dots", unit] += folded(weight * grad_prob, jnp.sum)

    def sums(unit):
        state["inverse", unit] = 1.0 / jnp.sum(state["total", unit], axis=0, keepdims=True)
        state["delta", unit] = jnp.sum(state["dots", unit], axis=0, keepdims=True) * state["inverse", unit]

    def prob_tile(unit, t):
        here = slice(t * high, (t + 1) * high)
        prob = pp_scr[unit % 4, here, :] * state["inverse", unit]
        p_scr[here, lanes(unit % 4)] = prob.astype(jnp.bfloat16)
        ds_scr[here, lanes(unit % 4)] = (prob * (dp_scr[unit % 4, here, :] - state["delta", unit])).astype(
            jnp.bfloat16
        )

    def products(unit):
        other, pair = units[unit]
        dscore, prob = ds_scr[:, lanes(unit % 4)], p_scr[:, lanes(unit % 4)]
        dq = jnp.dot(keys_t[other], dscore, preferred_element_type=jnp.float32).T * SCALE
        dq = dq.astype(jnp.bfloat16)
        dq_refs[other][:, 2 * pair * HD : (2 * pair + 1) * HD] = dq[:rows]
        dq_refs[other][:, (2 * pair + 1) * HD : (2 * pair + 2) * HD] = dq[rows:]
        key_part = jnp.dot(dscore, pair_of(q_refs, unit), preferred_element_type=jnp.float32)
        value_part = jnp.dot(prob, pair_of(g_refs, unit), preferred_element_type=jnp.float32)
        if pair == 0:
            key_acc[other] = key_part
            value_acc[other] = value_part
        else:
            key_acc[other] += key_part
            value_acc[other] += value_part

    scores(0)
    for t in tiles:
        weight_tile(0, t)
    sums(0)
    scores(1)
    for unit in range(len(units)):
        for t in tiles:
            prob_tile(unit, t)
            if unit + 1 < len(units):
                weight_tile(unit + 1, t)
        if unit + 1 < len(units):
            sums(unit + 1)
        if unit + 2 < len(units):
            scores(unit + 2)
        products(unit)

    acc[...] = jnp.zeros_like(acc)
    for other in range(2):
        here = pl.ds(pl.multiple_of(base[other], rows), width)
        acc[here, :HD] += key_acc[other] * SCALE
        acc[here, HD:] += value_acc[other]
    for which, y_rel, side in spots:
        parts[2 * which + y_rel][side * rows : (side + 1) * rows, :] = acc[spot(which, y_rel, side), :].astype(
            jnp.bfloat16
        )


def attention(lengths, queries, q_got, grad_out, g_got, pieces):
    rows, q_width = q_got.shape
    kv_heads = pieces[0].shape[1] // (2 * HD)
    span = q_width // kv_heads
    heads = span // HD
    width = (BACK + 1) * rows
    by_core = pl.BlockSpec((rows, span), lambda a: (0, kv_heads * (lax.axis_index("ctx") % 2) + a))
    by_head = pl.BlockSpec((rows, span), lambda a: (0, a))
    piece = pl.BlockSpec((2 * rows, 2 * HD), lambda a: (0, a))
    tile = pltpu.VMEM((heads // 2, width, 2 * rows), jnp.float32)
    flat = pltpu.VMEM((width, heads * rows), jnp.bfloat16)
    half = jax.ShapeDtypeStruct((rows, q_width), jnp.bfloat16)
    return pl.pallas_call(
        kernel,
        grid=(kv_heads,),
        in_specs=[
            pl.BlockSpec(lengths.shape, lambda a: (0, 0)),
            by_core,
            by_head,
            by_core,
            by_head,
            [piece] * 6,
        ],
        out_specs=[by_head, by_head, [piece] * 6],
        out_shape=[half, half, [jax.ShapeDtypeStruct(pieces[0].shape, jnp.bfloat16)] * 6],
        scratch_shapes=[
            pltpu.VMEM((12 * rows, 2 * HD), jnp.bfloat16),
            pltpu.VMEM((12 * rows, 2 * HD), jnp.float32),
            pltpu.VMEM((2, width, HD), jnp.float32),
            pltpu.VMEM((2, width, HD), jnp.float32),
            tile,
            tile,
            tile,
            flat,
            flat,
        ],
        compiler_params=pltpu.CompilerParams(vmem_limit_bytes=36 * 2**20),
    )(lengths, queries, q_got, grad_out, g_got, pieces)


def body(queries, keys, values, grad_out, doc_lengths):
    n_ctx = lax.axis_size("ctx")
    core = lax.axis_index("ctx") % 2
    swap_part = pairs(n_ctx, lambda g, c, y: (g, c, 1 - y))
    swap_core = pairs(n_ctx, lambda g, c, y: (g, 1 - c, y))
    rows, kv_width = keys.shape

    def sent(value, plan):
        return lax.ppermute(value, AXES, plan)

    def other_heads(value):
        half = value.shape[1] // 2
        return sent(lax.dynamic_slice_in_dim(value, (1 - core) * half, half, 1), swap_core)

    def in_order(mine, got, axis):
        return jnp.where(
            core == 0, jnp.concatenate([mine, got], axis=axis), jnp.concatenate([got, mine], axis=axis)
        )

    def added(*terms):
        return sum(term.astype(jnp.float32) for term in terms)

    chunk = jax.ShapeDtypeStruct(keys.shape, jnp.bfloat16)
    small = pltpu.CompilerParams(vmem_limit_bytes=4 * 2**20)
    mine, given = pl.pallas_call(
        split_kernel,
        out_shape=[chunk, chunk],
        compiler_params=pltpu.CompilerParams(vmem_limit_bytes=56 * 2**20),
    )(keys, values)
    own = in_order(mine, sent(given, swap_core), 0)
    far, near, beside = sent(own, ahead(n_ctx, 2)), sent(own, ahead(n_ctx, 1)), sent(own, swap_part)
    near, beside = lax.optimization_barrier((near, beside))
    pieces = [far, sent(far, swap_part), near, sent(near, swap_part), own, beside]
    dq_mine, dq_send, parts = attention(
        doc_lengths.reshape(1, -1), queries, other_heads(queries), grad_out, other_heads(grad_out), pieces
    )
    query_grad = in_order(dq_mine, sent(dq_send, swap_core), 1)
    total = None
    for which in range(3):
        summed = added(parts[2 * which], sent(parts[2 * which + 1], swap_part))
        if which < 2:
            summed = sent(summed.astype(jnp.bfloat16), ahead(n_ctx, which - 2))
            summed = summed.astype(jnp.float32)
        total = summed if total is None else total + summed
    total = total.astype(jnp.bfloat16)
    given = lax.dynamic_slice_in_dim(total, (1 - core) * rows, rows, 0)
    mine = lax.dynamic_slice_in_dim(total, core * rows, rows, 0)
    key_grad, value_grad = pl.pallas_call(merge_kernel, out_shape=[chunk, chunk], compiler_params=small)(mine, sent(given, swap_core))
    return query_grad, key_grad, value_grad


def solution(mesh):
    rows = P(AXES, None)
    return jax.shard_map(
        body,
        mesh=mesh,
        in_specs=(rows, rows, rows, rows, P()),
        out_specs=(rows, rows, rows),
        check_vma=False,
    )
```
